32 devices in a mesh: sec: 4 (over y, core), tile: 8 (over z, x).
Axes of the slice: x: 2, y: 2, z: 4, core: 2. Of those that a mesh axis runs over, the one named last changes fastest.
Arguments:
- offsets: float32 [2, 16, 64, 128], P(None, 'sec', 'tile'), may hold values from -6 to 6
- flow_tiles: float32 [16, 1024, 2, 128], P('sec', 'tile'), may hold values from -6 to 6
- confidence: float32 [16, 1024, 128], P('sec', 'tile'), may hold values from 0.1 to 10
- flow_owner: int32 [16, 1024, 1], P('sec', 'tile'), may hold values from 0 to 7; in each aligned block of 128 rows (0 to 127, 128 to 255, ..., all dimensions but the last counted through in order) at most 32 rows name the same one
- flow_row: int32 [16, 1024], P('sec', 'tile'), may hold values from 0 to 7
- match_up: int32 [16, 8, 1024], P('sec', 'tile'), may hold values from 0 to 1023, each once within a row
- match_down: int32 [16, 8, 1024], P('sec', 'tile'), may hold values from 0 to 1023, each once within a row
- classes: int32 [16, 64, 128], P('sec', 'tile'), may hold values from 0 to 3
- spring_table: float32 [2, 4], replicated, may hold values from 0.1 to 1
Outputs:
- position: float32 [2, 16, 64, 128], P(None, 'sec', 'tile')
- velocity: float32 [2, 16, 64, 128], P(None, 'sec', 'tile')
The draws below stay inside these ranges and needn't reach their ends.
Inputs may be any that keep to these rules, and one draw needn't show every extreme that they name: `flow_owner`: in each aligned block of 128 rows (the flow tiles of one section held by one image owner) no region is named more than 32 times, a bound that some block reaches. `match_up`: each row of 1024 entries names every node of a region once. `match_down`: each row of 1024 entries names every node of a region once.
All inputs are finite; a program needn't handle non-finite values.
Results may differ from the reference program's by a relative error of at most 0.000051.
Values sent between devices are 32-bit elements; how exact they have to be, the bound alone decides.
A program may use at most 64 MiB of HBM per device.

```python
import math
import jax
import jax.numpy as jnp
import numpy as np
from jax import lax

GX = 128
GY = 8
FT_DEV = 128
ITERS = 3
KCLASS = 4
OWNERS = 8
SECTIONS = 16
ROWS = 64
NODES = 1024
FLOWS = 1024
CAP = 32


def set_ends(values, stream_key, low, top_value):
    spot = [jax.random.randint(jax.random.fold_in(stream_key, axis), (), 0, length) for axis, length in enumerate(values.shape)]
    widest = values.shape.index(max(values.shape))
    neighbour = spot[:widest] + [(spot[widest] + 1) % values.shape[widest]] + spot[widest + 1:]
    return values.at[tuple(spot)].set(low).at[tuple(neighbour)].set(top_value)


def level_of(own_key, dims, split, low, top_value):
    def one(dim, blocks):
        draws = jax.random.uniform(jax.random.fold_in(jax.random.fold_in(own_key, 6), dim), (blocks,), jnp.float32, low / len(split), top_value / len(split))
        return jnp.repeat(jnp.exp(draws), dims[dim] // blocks).reshape((-1,) + (1,) * (len(dims) - dim - 1))

    loudness = one(*split[0])
    for cut in split[1:]:
        loudness = loudness * one(*cut)
    return loudness


def routed_block(own_key, own, number, rows, count, top, reach, lean):
    ranking = jax.random.permutation(own_key, count)
    packed, usual = shares(count, rows * top, reach, lean, True), shares(count, rows * top, reach, lean, False)
    places = jnp.arange(count)

    def named(lengths, turn):
        used = int((lengths > 0).sum())
        fixed = max(1, used // 4)
        shifted = fixed + (places - fixed + turn * (used - fixed)) % max(1, count - fixed)
        return jnp.zeros((count,), jnp.int32).at[ranking[jnp.where(places < fixed, places, shifted)]].set(jnp.asarray(lengths, jnp.int32))

    lengths = jnp.where(number % 4 == 0, named(packed, number // 4), named(usual, number - number // 4 - 1))
    mixed = jax.random.permutation(jax.random.fold_in(own, 3), count)
    source_of, taker = mixed[0:count // 2 * 2:2], mixed[1:count // 2 * 2:2]
    room = jnp.minimum(lengths[source_of] - 1, reach - lengths[taker]) // 2
    room = jnp.where((source_of == ranking[0]) | (taker == ranking[0]) | (lengths[taker] == 0), 0, jnp.maximum(room, 0))
    shifted = jax.random.randint(jax.random.fold_in(own, 4), (count // 2,), 0, 1 << 20) % (room + 1)
    lengths = lengths.at[source_of].add(-shifted).at[taker].add(shifted)
    members = jnp.searchsorted(jnp.cumsum(lengths), jnp.arange(rows * top), side="right").astype(jnp.int32)
    grid = members.reshape(top, rows).T
    grid = grid[jax.random.permutation(jax.random.fold_in(own, 1), rows)]
    turn = jax.random.randint(jax.random.fold_in(own, 2), (rows, 1), 0, top)
    return jnp.take_along_axis(grid, (jnp.arange(top)[None, :] + turn) % top, axis=1)


def shares(amount, total, bound, lean, full):
    loads = [(1 << 20) // math.isqrt(standing ** lean) + 1 for standing in range(1, amount + 1)]
    largest = bound if full else min(bound, max(-(-total // amount), total * loads[0] // sum(loads)))
    least = 1 if total - largest >= amount - 1 else 0
    counts, surplus = [largest] + [least] * (amount - 1), total - largest - least * (amount - 1)
    while surplus > 0:
        candidates = [i for i in range(1, amount) if counts[i] < largest] or [i for i in range(1, amount) if counts[i] < bound]
        pool, left = sum([loads[i] for i in candidates]), surplus
        for i in candidates:
            extra = min(bound - counts[i], max(1, left * loads[i] // pool), surplus)
            counts[i] = counts[i] + extra
            surplus = surplus - extra
    return np.array(counts)


def noise(stream_key, shape, spread, most, cuts=(), held_as=jnp.bfloat16):
    gain = level_of(stream_key, shape, cuts, -0.22, 0.18) if cuts else 1.0
    entries = jax.random.normal(stream_key, shape, jnp.float32) * spread * gain
    return jnp.minimum(jnp.maximum(entries, -most), most).astype(held_as)


def setup_inputs(seed: int = 0) -> dict:
    splits = jax.random.split(jax.random.key(seed), 10)
    offsets = noise(splits[0], (2, SECTIONS, ROWS, GX), 1.0, 6.0, ((1, 4), (2, 8)), jnp.float32)
    flow_tiles = noise(splits[1], (SECTIONS, FLOWS, 2, GX), 1.0, 6.0, ((0, 4), (1, 8)), jnp.float32)
    confidence = jnp.clip(jnp.exp(math.log(10.0) - 4.6051702 * jax.random.uniform(splits[2], (SECTIONS, FLOWS, GX), jnp.float32) ** level_of(splits[2], (SECTIONS, FLOWS, GX), ((0, 4), (1, 8)), -0.2, 0.2)), 0.1, 10.0)
    flow_owner_keys = jax.random.split(jax.random.fold_in(splits[3], 1), SECTIONS * FLOWS // FT_DEV)
    flow_owner_turns = jax.random.permutation(jax.random.fold_in(splits[3], 3), SECTIONS * FLOWS // FT_DEV)
    flow_owner = jax.vmap(lambda own, number: routed_block(jax.random.fold_in(splits[3], 2), own, number, FT_DEV, OWNERS, 1, CAP, 2))(flow_owner_keys, flow_owner_turns).reshape((SECTIONS, FLOWS, 1))
    flow_row = set_ends(jax.random.randint(splits[4], (SECTIONS, FLOWS), 0, GY), jax.random.fold_in(splits[4], 1), 0, GY - 1).astype(jnp.int32)
    match_up = jax.vmap(lambda own: jax.random.permutation(own, NODES))(jax.random.split(splits[5], SECTIONS * OWNERS)).reshape((SECTIONS, OWNERS, NODES)).astype(jnp.int32)
    match_down = jax.vmap(lambda own: jax.random.permutation(own, NODES))(jax.random.split(splits[6], SECTIONS * OWNERS)).reshape((SECTIONS, OWNERS, NODES)).astype(jnp.int32)
    classes = set_ends(jax.random.randint(splits[7], (SECTIONS, ROWS, GX), 0, KCLASS), jax.random.fold_in(splits[7], 1), 0, KCLASS - 1).astype(jnp.int32)
    spring_table = jnp.clip(jnp.exp(jax.random.uniform(splits[8], (2, KCLASS), jnp.float32, math.log(0.1), math.log(1.0))), 0.1, 1.0)
    return {"offsets": offsets, "flow_tiles": flow_tiles, "confidence": confidence, "flow_owner": flow_owner, "flow_row": flow_row, "match_up": match_up, "match_down": match_down, "classes": classes, "spring_table": spring_table}


def stiffness_of(classes, spring_table):
    k_plane = jnp.zeros(classes.shape, jnp.float32)
    k_cross = jnp.zeros(classes.shape, jnp.float32)
    for class_id in range(spring_table.shape[1]):
        class_hit = (classes == class_id).astype(jnp.float32)
        k_plane = k_plane + class_hit * spring_table[0, class_id]
        k_cross = k_cross + class_hit * spring_table[1, class_id]
    return k_plane, k_cross


def reference(offsets, flow_tiles, confidence, flow_owner, flow_row, match_up, match_down, classes, spring_table):
    payload = jnp.concatenate([flow_tiles * confidence[:, :, None, :], confidence[:, :, None, :]], axis=2)
    payload = payload.reshape(SECTIONS, FLOWS, 3 * GX)
    row_key = (flow_owner[:, :, 0] * GY + flow_row).astype(jnp.int32)

    def collect(section):
        rows_of, keys_of = section
        return jax.ops.segment_sum(rows_of, keys_of, num_segments=ROWS)

    gathered = lax.map(collect, (payload, row_key)).reshape(SECTIONS, ROWS, 3, GX)
    pulled_sum = jnp.moveaxis(gathered[:, :, :2], 2, 0)
    weight_sum = gathered[:, :, 2]
    k_plane, k_cross = stiffness_of(classes, spring_table)
    position = offsets
    velocity = jnp.zeros(offsets.shape, jnp.float32)
    empty = jnp.zeros((2, 1, ROWS, GX), jnp.float32)
    up_index = jnp.broadcast_to(match_up[None], (2,) + match_up.shape)
    down_index = jnp.broadcast_to(match_down[None], (2,) + match_down.shape)
    for sweep in range(ITERS):
        padded = jnp.pad(position, ((0, 0), (0, 0), (1, 1), (1, 1)))
        laplace = padded[:, :, 2:, 1:-1] + padded[:, :, :-2, 1:-1] + padded[:, :, 1:-1, 2:] + padded[:, :, 1:-1, :-2] - 4.0 * position
        above_sec = jnp.concatenate([position[:, 1:], empty], axis=1)
        below_sec = jnp.concatenate([empty, position[:, :-1]], axis=1)
        up_pulled = jnp.take_along_axis(above_sec.reshape(2, SECTIONS, OWNERS, NODES), up_index, axis=3).reshape(position.shape)
        down_pulled = jnp.take_along_axis(below_sec.reshape(2, SECTIONS, OWNERS, NODES), down_index, axis=3).reshape(position.shape)
        net_force = k_plane * laplace + k_cross * (up_pulled + down_pulled - 2.0 * position) + (pulled_sum - weight_sum * position) / (1.0 + weight_sum)
        velocity = 0.9 * velocity + 0.5 * net_force
        position = position + 0.5 * velocity
    return position, velocity
```

```python
import functools

import jax
import jax.numpy as jnp
from jax import lax
from jax.experimental import pallas as pl
from jax.experimental.pallas import tpu as pltpu
from jax.sharding import PartitionSpec as P

ITERS = 3


def gather_nodes(source, row, col):
    rows = source.shape[0]
    picked = None
    for r in range(rows):
        line = jnp.broadcast_to(source[r : r + 1, :], source.shape)
        taken = jnp.take_along_axis(line, col, axis=1)
        picked = taken if r == 0 else jnp.where(row == r, taken, picked)
    return picked


def kernel(
    n_tile,
    n_sec,
    offsets,
    flow,
    conf,
    owner,
    flow_row,
    match_up,
    match_down,
    classes,
    table,
    pos_out,
    vel_out,
    dense,
    near_other,
    near_own,
    crossing,
    crossed,
    pos,
    vel,
    edge_out,
    edge_in,
    near_send,
    near_recv,
    cross_send,
    cross_recv,
    tile_send,
    tile_recv,
    sec_send,
    sec_recv,
):
    comps, secs, rows, cols = offsets.shape
    flows = conf.shape[1]
    half = n_tile // 2
    t = lax.axis_index("tile")
    s_me = lax.axis_index("sec")
    h, j = t // half, t % half

    barrier = pltpu.get_barrier_semaphore()
    for d in range(1, n_tile):
        pl.semaphore_signal(barrier, inc=1, device_id={"tile": (t + d) % n_tile})
    has_prev, has_next = s_me > 0, s_me < n_sec - 1
    has_left, has_right = t > 0, t < n_tile - 1

    for d in (1, n_sec - 1):
        pl.semaphore_signal(barrier, inc=1, device_id={"sec": (s_me + d) % n_sec})

    zero = jnp.zeros((rows, cols), jnp.float32)
    for s in range(secs):
        for c in range(comps):
            here = offsets[c, s]
            pos[0, s + 1, c] = here
            edge_out[0, 0, c * secs + s : c * secs + s + 1, :] = here[:1]
            edge_out[0, 1, c * secs + s : c * secs + s + 1, :] = here[rows - 1 :]

    key_iota = lax.broadcasted_iota(jnp.int32, (n_tile * rows, flows), 0)
    for s in range(secs):
        key = owner[s : s + 1, :] * rows + flow_row[s : s + 1, :]
        hit = (jnp.broadcast_to(key, key_iota.shape) == key_iota).astype(jnp.float32)
        hit = hit.astype(jnp.bfloat16)
        w = conf[s]
        parts = [w * flow[s, pl.ds(c, flows, stride=comps), :] for c in range(comps)] + [w]
        payload = jnp.concatenate(parts, axis=1)
        high = payload.astype(jnp.bfloat16)
        low = (payload - high.astype(jnp.float32)).astype(jnp.bfloat16)
        both = jnp.concatenate([high, low], axis=0)
        hit2 = jnp.concatenate([hit, hit], axis=1)
        sums = jnp.dot(hit2, both, preferred_element_type=jnp.float32)
        for o in range(n_tile):
            for c in range(comps + 1):
                dense[o, s, c] = sums[o * rows : (o + 1) * rows, c * cols : (c + 1) * cols]

    pl.semaphore_wait(barrier, n_tile + 1)

    def sec_copy(k, up):
        return pltpu.make_async_remote_copy(
            src_ref=pos.at[k, 1 if up else secs],
            dst_ref=pos.at[k, secs + 1 if up else 0],
            send_sem=sec_send.at[k, 0 if up else 1],
            recv_sem=sec_recv.at[k, 0 if up else 1],
            device_id={"sec": s_me - 1 if up else s_me + 1},
        )

    def tile_copy(k, up):
        return pltpu.make_async_remote_copy(
            src_ref=edge_out.at[k, 0 if up else 1],
            dst_ref=edge_in.at[k, 1 if up else 0],
            send_sem=tile_send.at[k, 0 if up else 1],
            recv_sem=tile_recv.at[k, 0 if up else 1],
            device_id={"tile": t - 1 if up else t + 1},
        )

    def near_copy(d, part):
        to = (j + d) % half
        source = dense.at[(1 - h if part == 0 else h) * half + to]
        landing = near_other if part == 0 else near_own
        return pltpu.make_async_remote_copy(
            src_ref=source,
            dst_ref=landing.at[d - 1],
            send_sem=near_send.at[part, d - 1],
            recv_sem=near_recv.at[part, d - 1],
            device_id={"tile": h * half + to},
        )

    cross = pltpu.make_async_remote_copy(
        src_ref=crossing,
        dst_ref=crossed,
        send_sem=cross_send,
        recv_sem=cross_recv,
        device_id={"tile": (1 - h) * half + j},
    )

    def start_halo(k):
        pl.when(has_prev)(lambda: sec_copy(k, True).start())
        pl.when(has_next)(lambda: sec_copy(k, False).start())
        pl.when(has_left)(lambda: tile_copy(k, True).start())
        pl.when(has_right)(lambda: tile_copy(k, False).start())

    def wait_halo(k):
        @pl.when(has_prev)
        def _():
            sec_copy(k, True).wait_send()
            sec_copy(k, False).wait_recv()

        @pl.when(has_next)
        def _():
            sec_copy(k, False).wait_send()
            sec_copy(k, True).wait_recv()

        @pl.when(has_left)
        def _():
            tile_copy(k, True).wait_send()
            tile_copy(k, False).wait_recv()

        @pl.when(has_right)
        def _():
            tile_copy(k, False).wait_send()
            tile_copy(k, True).wait_recv()

    for d in range(1, half):
        near_copy(d, 0).start()
    start_halo(0)

    for k in range(ITERS):

        @pl.when(jnp.logical_not(has_prev))
        def _():
            for c in range(comps):
                pos[k, 0, c] = zero

        @pl.when(jnp.logical_not(has_next))
        def _():
            for c in range(comps):
                pos[k, secs + 1, c] = zero

        @pl.when(jnp.logical_not(has_left))
        def _():
            edge_in[k, 0] = jnp.zeros(edge_in.shape[2:], jnp.float32)

        @pl.when(jnp.logical_not(has_right))
        def _():
            edge_in[k, 1] = jnp.zeros(edge_in.shape[2:], jnp.float32)

    row_iota = lax.broadcasted_iota(jnp.int32, (rows, cols), 0)
    col_iota = lax.broadcasted_iota(jnp.int32, (rows, cols), 1)
    k_plane, k_cross = [], []
    for s in range(secs):
        kind = classes[s]
        plane, across = zero, zero
        for class_id in range(table.shape[1]):
            plane = jnp.where(kind == class_id, table[0, class_id], plane)
            across = jnp.where(kind == class_id, table[1, class_id], across)
        k_plane.append(plane)
        k_cross.append(across)

    def pulled(k, s, c, up):
        index = (match_up if up else match_down)[s]
        source = pos[k, s + 2 if up else s, c]
        return gather_nodes(source, index // cols, index % cols)

    def local_force(k, s, c):
        here = pos[k, s + 1, c]
        west = jnp.where(col_iota == 0, 0.0, pltpu.roll(here, 1, 1))
        east = jnp.where(col_iota == cols - 1, 0.0, pltpu.roll(here, cols - 1, 1))
        north = jnp.where(row_iota == 0, 0.0, pltpu.roll(here, 1, 0))
        south = jnp.where(row_iota == rows - 1, 0.0, pltpu.roll(here, rows - 1, 0))
        force = k_plane[s] * (west + east + north + south - 4.0 * here) - 2.0 * k_cross[s] * here
        if s < secs - 1:
            force = force + k_cross[s] * pulled(k, s, c, True)
        if s > 0:
            force = force + k_cross[s] * pulled(k, s, c, False)
        return force

    def halo_force(k, s, c):
        line = c * secs + s
        north = jnp.where(row_iota == 0, edge_in[k, 0, line : line + 1, :], 0.0)
        south = jnp.where(row_iota == rows - 1, edge_in[k, 1, line : line + 1, :], 0.0)
        force = k_plane[s] * (north + south)
        if s == secs - 1:
            force = force + k_cross[s] * pulled(k, s, c, True)
        if s == 0:
            force = force + k_cross[s] * pulled(k, s, c, False)
        return force

    nodes = [(s, c) for s in [0, secs - 1] + list(range(1, secs - 1)) for c in range(comps)]

    for k in range(ITERS):
        force = {(s, c): local_force(k, s, c) for s, c in nodes}
        if k == 0:
            wait_halo(0)
            force = {(s, c): force[s, c] + halo_force(0, s, c) for s, c in nodes}
            for d in range(1, half):
                near_copy(d, 0).wait_recv()
            for s in range(secs):
                for c in range(comps + 1):
                    total = dense[(1 - h) * half + j, s, c]
                    for d in range(1, half):
                        total = total + near_other[d - 1, s, c]
                    crossing[s, c] = total
            cross.start()
            for d in range(1, half):
                near_copy(d, 1).start()
            for d in range(1, half):
                near_copy(d, 1).wait_recv()
            cross.wait_recv()
            flow_push, flow_hold = {}, {}
            for s in range(secs):
                sums = []
                for c in range(comps + 1):
                    total = dense[t, s, c] + crossed[s, c]
                    for d in range(1, half):
                        total = total + near_own[d - 1, s, c]
                    sums.append(total)
                scale = 1.0 / (1.0 + sums[comps])
                flow_hold[s] = sums[comps] * scale
                for c in range(comps):
                    flow_push[s, c] = sums[c] * scale
        else:
            wait_halo(k)
            force = {(s, c): force[s, c] + halo_force(k, s, c) for s, c in nodes}
        for s, c in nodes:
            here = pos[k, s + 1, c]
            net = force[s, c] + flow_push[s, c] - flow_hold[s] * here
            speed = 0.5 * net if k == 0 else 0.9 * vel[s, c] + 0.5 * net
            moved = here + 0.5 * speed
            if k < ITERS - 1:
                vel[s, c] = speed
                pos[k + 1, s + 1, c] = moved
                line = c * secs + s
                edge_out[k + 1, 0, line : line + 1, :] = moved[:1]
                edge_out[k + 1, 1, line : line + 1, :] = moved[rows - 1 :]
            else:
                vel_out[c, s] = speed
                pos_out[c, s] = moved
        if k < ITERS - 1:
            start_halo(k + 1)
        if k == 0:
            for d in range(1, half):
                near_copy(d, 0).wait_send()
                near_copy(d, 1).wait_send()
            cross.wait_send()


def shards(n_tile, n_sec, *args):
    offsets, flow_tiles, confidence, flow_owner, flow_row = args[:5]
    match_up, match_down, classes, spring_table = args[5:]
    comps, secs, rows, cols = offsets.shape
    flows = confidence.shape[1]
    half = n_tile // 2
    block = (secs, comps + 1, rows, cols)
    vmem = pl.BlockSpec(memory_space=pltpu.VMEM)
    f32 = jnp.float32
    dma = pltpu.SemaphoreType.DMA
    out = jax.ShapeDtypeStruct(offsets.shape, f32)
    return pl.pallas_call(
        functools.partial(kernel, n_tile, n_sec),
        out_shape=(out, out),
        in_specs=[vmem] * 8 + [pl.BlockSpec(memory_space=pltpu.SMEM)],
        out_specs=(vmem, vmem),
        scratch_shapes=[
            pltpu.VMEM((n_tile,) + block, f32),
            pltpu.VMEM((half - 1,) + block, f32),
            pltpu.VMEM((half - 1,) + block, f32),
            pltpu.VMEM(block, f32),
            pltpu.VMEM(block, f32),
            pltpu.VMEM((ITERS, secs + 2, comps, rows, cols), f32),
            pltpu.VMEM((secs, comps, rows, cols), f32),
            pltpu.VMEM((ITERS, 2, comps * secs, cols), f32),
            pltpu.VMEM((ITERS, 2, comps * secs, cols), f32),
            dma((2, half - 1)),
            dma((2, half - 1)),
            dma,
            dma,
            dma((ITERS, 2)),
            dma((ITERS, 2)),
            dma((ITERS, 2)),
            dma((ITERS, 2)),
        ],
        compiler_params=pltpu.CompilerParams(
            collective_id=0, has_side_effects=True, vmem_limit_bytes=32 * 1024 * 1024
        ),
    )(
        offsets,
        flow_tiles.reshape(secs, flows * comps, cols),
        confidence,
        flow_owner.reshape(secs, flows),
        flow_row,
        match_up.reshape(secs, rows, cols),
        match_down.reshape(secs, rows, cols),
        classes,
        spring_table,
    )


def solution(mesh):
    placed = (
        P(None, "sec", "tile", None),
        P("sec", "tile", None, None),
        P("sec", "tile", None),
        P("sec", "tile", None),
        P("sec", "tile"),
        P("sec", "tile", None),
        P("sec", "tile", None),
        P("sec", "tile", None),
        P(),
    )
    return jax.shard_map(
        functools.partial(shards, mesh.shape["tile"], mesh.shape["sec"]),
        mesh=mesh,
        in_specs=placed,
        out_specs=(P(None, "sec", "tile", None), P(None, "sec", "tile", None)),
        check_vma=False,
    )
```

```python
import functools

import jax
import jax.numpy as jnp
from jax import lax
from jax.experimental import pallas as pl
from jax.experimental.pallas import tpu as pltpu
from jax.sharding import PartitionSpec as P

ITERS = 3
CHUNKS = 2


def gather_nodes(source, row, col):
    rows = source.shape[0]
    picked = None
    for r in range(rows):
        line = jnp.broadcast_to(source[r : r + 1, :], source.shape)
        taken = jnp.take_along_axis(line, col, axis=1)
        picked = taken if r == 0 else jnp.where(row == r, taken, picked)
    return picked


def kernel(
    n_tile,
    n_sec,
    *refs,
):
    in_hbm, outs, staged = refs[:9], refs[9:12], refs[12:21]
    offsets, flow, conf, owner, flow_row, match_up, match_down, classes, table = staged
    net_out, vel_out, pos_out = outs
    dense, near_other, near_own, crossing, crossed, pos, vel, edge_out, edge_in = refs[21:30]
    near_send, near_recv, cross_send, cross_recv = refs[30:34]
    tile_send, tile_recv, sec_send, sec_recv, load_sem, part_sem = refs[34:]
    comps, secs, rows, cols = offsets.shape
    flows = conf.shape[1]
    half = n_tile // 2
    t = lax.axis_index("tile")
    s_me = lax.axis_index("sec")
    h, j = t // half, t % half

    chunks = min(CHUNKS, secs)
    step = secs // chunks

    def load(i):
        return pltpu.make_async_copy(in_hbm[i], staged[i], load_sem.at[i])

    def load_part(i, s):
        return pltpu.make_async_copy(in_hbm[i].at[s], staged[i].at[s], part_sem.at[i - 1, s])

    load(3).start()
    load(4).start()
    for s in range(secs):
        load_part(1, s).start()
        load_part(2, s).start()
    for i in (0, 5, 6, 7, 8):
        load(i).start()

    barrier = pltpu.get_barrier_semaphore()
    for d in range(1, n_tile):
        pl.semaphore_signal(barrier, inc=1, device_id={"tile": (t + d) % n_tile})
    has_prev, has_next = s_me > 0, s_me < n_sec - 1
    has_left, has_right = t > 0, t < n_tile - 1

    for d in (1, n_sec - 1):
        pl.semaphore_signal(barrier, inc=1, device_id={"sec": (s_me + d) % n_sec})

    key_iota = lax.broadcasted_iota(jnp.int32, (n_tile * rows, flows), 0)

    def segment_sums(s):
        load_part(1, s).wait()
        load_part(2, s).wait()
        key = owner[s : s + 1, :] * rows + flow_row[s : s + 1, :]
        hit = (jnp.broadcast_to(key, key_iota.shape) == key_iota).astype(jnp.float32)
        hit = hit.astype(jnp.bfloat16)
        w = conf[s]
        parts = [w * flow[s, pl.ds(c, flows, stride=comps), :] for c in range(comps)] + [w]
        payload = jnp.concatenate(parts, axis=1)
        high = payload.astype(jnp.bfloat16)
        low = (payload - high.astype(jnp.float32)).astype(jnp.bfloat16)
        both = jnp.concatenate([high, low], axis=0)
        hit2 = jnp.concatenate([hit, hit], axis=1)
        sums = jnp.dot(hit2, both, preferred_element_type=jnp.float32)
        for o in range(n_tile):
            for c in range(comps + 1):
                dense[o, s, c] = sums[o * rows : (o + 1) * rows, c * cols : (c + 1) * cols]

    def sec_copy(k, up):
        return pltpu.make_async_remote_copy(
            src_ref=pos.at[k, 1 if up else secs],
            dst_ref=pos.at[k, secs + 1 if up else 0],
            send_sem=sec_send.at[k, 0 if up else 1],
            recv_sem=sec_recv.at[k, 0 if up else 1],
            device_id={"sec": s_me - 1 if up else s_me + 1},
        )

    def tile_copy(k, up):
        return pltpu.make_async_remote_copy(
            src_ref=edge_out.at[k, 0 if up else 1],
            dst_ref=edge_in.at[k, 1 if up else 0],
            send_sem=tile_send.at[k, 0 if up else 1],
            recv_sem=tile_recv.at[k, 0 if up else 1],
            device_id={"tile": t - 1 if up else t + 1},
        )

    def near_copy(d, part, m):
        to = (j + d) % half
        source = dense.at[(1 - h if part == 0 else h) * half + to]
        landing = near_other if part == 0 else near_own
        return pltpu.make_async_remote_copy(
            src_ref=source.at[pl.ds(m * step, step)],
            dst_ref=landing.at[d - 1, pl.ds(m * step, step)],
            send_sem=near_send.at[part, d - 1, m],
            recv_sem=near_recv.at[part, d - 1, m],
            device_id={"tile": h * half + to},
        )

    def cross_copy(m):
        return pltpu.make_async_remote_copy(
            src_ref=crossing.at[pl.ds(m * step, step)],
            dst_ref=crossed.at[pl.ds(m * step, step)],
            send_sem=cross_send.at[m],
            recv_sem=cross_recv.at[m],
            device_id={"tile": (1 - h) * half + j},
        )

    def start_halo(k):
        pl.when(has_prev)(lambda: sec_copy(k, True).start())
        pl.when(has_next)(lambda: sec_copy(k, False).start())
        pl.when(has_left)(lambda: tile_copy(k, True).start())
        pl.when(has_right)(lambda: tile_copy(k, False).start())

    def wait_halo(k):
        @pl.when(has_prev)
        def _():
            sec_copy(k, True).wait_send()
            sec_copy(k, False).wait_recv()

        @pl.when(has_next)
        def _():
            sec_copy(k, False).wait_send()
            sec_copy(k, True).wait_recv()

        @pl.when(has_left)
        def _():
            tile_copy(k, True).wait_send()
            tile_copy(k, False).wait_recv()

        @pl.when(has_right)
        def _():
            tile_copy(k, False).wait_send()
            tile_copy(k, True).wait_recv()

    load(3).wait()
    load(4).wait()
    for m in range(chunks):
        for s in range(m * step, (m + 1) * step):
            segment_sums(s)
        if m == 0:
            pl.semaphore_wait(barrier, n_tile + 1)
        for d in range(1, half):
            near_copy(d, 0, m).start()
    load(0).wait()
    for s in range(secs):
        for c in range(comps):
            here = offsets[c, s]
            pos[0, s + 1, c] = here
            edge_out[0, 0, c * secs + s : c * secs + s + 1, :] = here[:1]
            edge_out[0, 1, c * secs + s : c * secs + s + 1, :] = here[rows - 1 :]
    start_halo(0)
    zero = jnp.zeros((rows, cols), jnp.float32)

    for k in range(ITERS):

        @pl.when(jnp.logical_not(has_prev))
        def _():
            for c in range(comps):
                pos[k, 0, c] = zero

        @pl.when(jnp.logical_not(has_next))
        def _():
            for c in range(comps):
                pos[k, secs + 1, c] = zero

        @pl.when(jnp.logical_not(has_left))
        def _():
            edge_in[k, 0] = jnp.zeros(edge_in.shape[2:], jnp.float32)

        @pl.when(jnp.logical_not(has_right))
        def _():
            edge_in[k, 1] = jnp.zeros(edge_in.shape[2:], jnp.float32)

    for i in (5, 6, 7, 8):
        load(i).wait()
    row_iota = lax.broadcasted_iota(jnp.int32, (rows, cols), 0)
    col_iota = lax.broadcasted_iota(jnp.int32, (rows, cols), 1)
    k_plane, k_cross = [], []
    for s in range(secs):
        kind = classes[s]
        plane, across = zero, zero
        for class_id in range(table.shape[1]):
            plane = jnp.where(kind == class_id, table[0:1, class_id : class_id + 1], plane)
            across = jnp.where(kind == class_id, table[1:2, class_id : class_id + 1], across)
        k_plane.append(plane)
        k_cross.append(across)

    def pulled(k, s, c, up):
        index = (match_up if up else match_down)[s]
        source = pos[k, s + 2 if up else s, c]
        return gather_nodes(source, index // cols, index % cols)

    def local_force(k, s, c):
        here = pos[k, s + 1, c]
        west = jnp.where(col_iota == 0, 0.0, pltpu.roll(here, 1, 1))
        east = jnp.where(col_iota == cols - 1, 0.0, pltpu.roll(here, cols - 1, 1))
        north = jnp.where(row_iota == 0, 0.0, pltpu.roll(here, 1, 0))
        south = jnp.where(row_iota == rows - 1, 0.0, pltpu.roll(here, rows - 1, 0))
        force = k_plane[s] * (west + east + north + south - 4.0 * here) - 2.0 * k_cross[s] * here
        if s < secs - 1:
            force = force + k_cross[s] * pulled(k, s, c, True)
        if s > 0:
            force = force + k_cross[s] * pulled(k, s, c, False)
        return force

    def halo_force(k, s, c):
        line = c * secs + s
        north = jnp.where(row_iota == 0, edge_in[k, 0, line : line + 1, :], 0.0)
        south = jnp.where(row_iota == rows - 1, edge_in[k, 1, line : line + 1, :], 0.0)
        force = k_plane[s] * (north + south)
        if s == secs - 1:
            force = force + k_cross[s] * pulled(k, s, c, True)
        if s == 0:
            force = force + k_cross[s] * pulled(k, s, c, False)
        return force

    nodes = [(s, c) for s in [0, secs - 1] + list(range(1, secs - 1)) for c in range(comps)]

    for k in range(ITERS):
        force = {(s, c): local_force(k, s, c) for s, c in nodes}
        if k == 0:
            for m in range(chunks):
                for d in range(1, half):
                    near_copy(d, 0, m).wait_recv()
                for s in range(m * step, (m + 1) * step):
                    for c in range(comps + 1):
                        total = dense[(1 - h) * half + j, s, c]
                        for d in range(1, half):
                            total = total + near_other[d - 1, s, c]
                        crossing[s, c] = total
                cross_copy(m).start()
            for m in range(chunks):
                for d in range(1, half):
                    near_copy(d, 1, m).start()
            wait_halo(0)
            force = {(s, c): force[s, c] + halo_force(0, s, c) for s, c in nodes}
            for m in range(chunks):
                for d in range(1, half):
                    near_copy(d, 1, m).wait_recv()
                cross_copy(m).wait_recv()
            flow_push, flow_hold = {}, {}
            for s in range(secs):
                sums = []
                for c in range(comps + 1):
                    total = dense[t, s, c] + crossed[s, c]
                    for d in range(1, half):
                        total = total + near_own[d - 1, s, c]
                    sums.append(total)
                scale = 1.0 / (1.0 + sums[comps])
                flow_hold[s] = sums[comps] * scale
                for c in range(comps):
                    flow_push[s, c] = sums[c] * scale
        else:
            wait_halo(k)
            force = {(s, c): force[s, c] + halo_force(k, s, c) for s, c in nodes}
        for s, c in nodes:
            here = pos[k, s + 1, c]
            net = force[s, c] + flow_push[s, c] - flow_hold[s] * here
            if k == ITERS - 1:
                net_out[c, s] = net
                vel_out[c, s] = vel[s, c]
                pos_out[c, s] = here
                continue
            speed = 0.5 * net if k == 0 else 0.9 * vel[s, c] + 0.5 * net
            moved = here + 0.5 * speed
            vel[s, c] = speed
            pos[k + 1, s + 1, c] = moved
            line = c * secs + s
            edge_out[k + 1, 0, line : line + 1, :] = moved[:1]
            edge_out[k + 1, 1, line : line + 1, :] = moved[rows - 1 :]
        if k < ITERS - 1:
            start_halo(k + 1)
        if k == 0:
            for m in range(chunks):
                for d in range(1, half):
                    near_copy(d, 0, m).wait_send()
                    near_copy(d, 1, m).wait_send()
                cross_copy(m).wait_send()


def shards(n_tile, n_sec, *args):
    offsets, flow_tiles, confidence, flow_owner, flow_row = args[:5]
    match_up, match_down, classes, spring_table = args[5:]
    comps, secs, rows, cols = offsets.shape
    flows = confidence.shape[1]
    half = n_tile // 2
    block = (secs, comps + 1, rows, cols)
    vmem = pl.BlockSpec(memory_space=pltpu.VMEM)
    f32 = jnp.float32
    dma = pltpu.SemaphoreType.DMA
    out = jax.ShapeDtypeStruct(offsets.shape, f32)
    chunks = min(CHUNKS, secs)
    operands = (
        offsets,
        flow_tiles.reshape(secs, flows * comps, cols),
        confidence,
        flow_owner.reshape(secs, flows),
        flow_row,
        match_up.reshape(secs, rows, cols),
        match_down.reshape(secs, rows, cols),
        classes,
        spring_table,
    )
    net, velocity, position = pl.pallas_call(
        functools.partial(kernel, n_tile, n_sec),
        out_shape=(out, out, out),
        in_specs=[pl.BlockSpec(memory_space=pltpu.HBM)] * 9,
        out_specs=(vmem, vmem, vmem),
        scratch_shapes=[pltpu.VMEM(x.shape, x.dtype) for x in operands]
        + [
            pltpu.VMEM((n_tile,) + block, f32),
            pltpu.VMEM((half - 1,) + block, f32),
            pltpu.VMEM((half - 1,) + block, f32),
            pltpu.VMEM(block, f32),
            pltpu.VMEM(block, f32),
            pltpu.VMEM((ITERS, secs + 2, comps, rows, cols), f32),
            pltpu.VMEM((secs, comps, rows, cols), f32),
            pltpu.VMEM((ITERS, 2, comps * secs, cols), f32),
            pltpu.VMEM((ITERS, 2, comps * secs, cols), f32),
            dma((2, half - 1, chunks)),
            dma((2, half - 1, chunks)),
            dma((chunks,)),
            dma((chunks,)),
            dma((ITERS, 2)),
            dma((ITERS, 2)),
            dma((ITERS, 2)),
            dma((ITERS, 2)),
            dma((9,)),
            dma((2, secs)),
        ],
        compiler_params=pltpu.CompilerParams(
            collective_id=0, has_side_effects=True, vmem_limit_bytes=63 * 1024 * 1024
        ),
    )(*operands)
    velocity = 0.9 * velocity + 0.5 * net
    return position + 0.5 * velocity, velocity


def solution(mesh):
    placed = (
        P(None, "sec", "tile", None),
        P("sec", "tile", None, None),
        P("sec", "tile", None),
        P("sec", "tile", None),
        P("sec", "tile"),
        P("sec", "tile", None),
        P("sec", "tile", None),
        P("sec", "tile", None),
        P(),
    )
    return jax.shard_map(
        functools.partial(shards, mesh.shape["tile"], mesh.shape["sec"]),
        mesh=mesh,
        in_specs=placed,
        out_specs=(P(None, "sec", "tile", None), P(None, "sec", "tile", None)),
        check_vma=False,
    )
```

```python
import functools

import jax
import jax.numpy as jnp
from jax import lax
from jax.experimental import pallas as pl
from jax.experimental.pallas import tpu as pltpu
from jax.sharding import PartitionSpec as P

ITERS = 3
CHUNKS = 1


def gather_nodes(source, row, col):
    rows = source.shape[0]
    picked = None
    for r in range(rows):
        line = jnp.broadcast_to(source[r : r + 1, :], source.shape)
        taken = jnp.take_along_axis(line, col, axis=1)
        picked = taken if r == 0 else jnp.where(row == r, taken, picked)
    return picked


def kernel(
    n_tile,
    n_sec,
    *refs,
):
    in_hbm, outs, staged = refs[:9], refs[9:12], refs[12:21]
    offsets, flow, conf, owner, flow_row, match_up, match_down, classes, table = staged
    net_out, vel_out, pos_out = outs
    dense, near_other, near_own, crossing, crossed, pos, vel, edge_out, edge_in = refs[21:30]
    near_send, near_recv, cross_send, cross_recv = refs[30:34]
    tile_send, tile_recv, sec_send, sec_recv, load_sem, part_sem = refs[34:]
    comps, secs, rows, cols = offsets.shape
    flows = conf.shape[1]
    half = n_tile // 2
    t = lax.axis_index("tile")
    s_me = lax.axis_index("sec")
    h, j = t // half, t % half

    chunks = min(CHUNKS, secs)
    step = secs // chunks

    def load(i):
        return pltpu.make_async_copy(in_hbm[i], staged[i], load_sem.at[i])

    def load_part(i, s):
        return pltpu.make_async_copy(in_hbm[i].at[s], staged[i].at[s], part_sem.at[i - 1, s])

    load(3).start()
    load(4).start()
    for s in range(secs):
        load_part(1, s).start()
        load_part(2, s).start()
    for i in (0, 5, 6, 7, 8):
        load(i).start()

    barrier = pltpu.get_barrier_semaphore()
    has_prev, has_next = s_me > 0, s_me < n_sec - 1
    has_left, has_right = t > 0, t < n_tile - 1

    for d in range(1, half):
        pl.semaphore_signal(barrier, inc=1, device_id={"tile": h * half + (j + d) % half})
    pl.semaphore_signal(barrier, inc=1, device_id={"tile": (1 - h) * half + j})
    over_right = jnp.logical_and(t == half - 1, half > 1)
    over_left = jnp.logical_and(t == half, half > 1)

    def greet(there, partner):
        @pl.when(there)
        def _():
            pl.semaphore_signal(barrier, inc=1, device_id=partner)

    greet(has_prev, {"sec": s_me - 1})
    greet(has_next, {"sec": s_me + 1})
    greet(over_right, {"tile": t + 1})
    greet(over_left, {"tile": t - 1})
    partners = half
    for there in (has_prev, has_next, over_right, over_left):
        partners = partners + there.astype(jnp.int32)

    key_iota = lax.broadcasted_iota(jnp.int32, (n_tile * rows, flows), 0)

    def segment_sums(s):
        load_part(1, s).wait()
        load_part(2, s).wait()
        key = owner[s : s + 1, :] * rows + flow_row[s : s + 1, :]
        hit = (jnp.broadcast_to(key, key_iota.shape) == key_iota).astype(jnp.float32)
        hit = hit.astype(jnp.bfloat16)
        w = conf[s]
        parts = [w * flow[s, pl.ds(c, flows, stride=comps), :] for c in range(comps)] + [w]
        payload = jnp.concatenate(parts, axis=1)
        high = payload.astype(jnp.bfloat16)
        low = (payload - high.astype(jnp.float32)).astype(jnp.bfloat16)
        both = jnp.concatenate([high, low], axis=0)
        hit2 = jnp.concatenate([hit, hit], axis=1)
        sums = jnp.dot(hit2, both, preferred_element_type=jnp.float32)
        for o in range(n_tile):
            for c in range(comps + 1):
                dense[o, s, c] = sums[o * rows : (o + 1) * rows, c * cols : (c + 1) * cols]

    def sec_copy(k, up):
        return pltpu.make_async_remote_copy(
            src_ref=pos.at[k, 1 if up else secs],
            dst_ref=pos.at[k, secs + 1 if up else 0],
            send_sem=sec_send.at[k, 0 if up else 1],
            recv_sem=sec_recv.at[k, 0 if up else 1],
            device_id={"sec": s_me - 1 if up else s_me + 1},
        )

    def tile_copy(k, up):
        return pltpu.make_async_remote_copy(
            src_ref=edge_out.at[k, 0 if up else 1],
            dst_ref=edge_in.at[k, 1 if up else 0],
            send_sem=tile_send.at[k, 0 if up else 1],
            recv_sem=tile_recv.at[k, 0 if up else 1],
            device_id={"tile": t - 1 if up else t + 1},
        )

    def near_copy(d, part, m):
        to = (j + d) % half
        source = dense.at[(1 - h if part == 0 else h) * half + to]
        landing = near_other if part == 0 else near_own
        return pltpu.make_async_remote_copy(
            src_ref=source.at[pl.ds(m * step, step)],
            dst_ref=landing.at[d - 1, pl.ds(m * step, step)],
            send_sem=near_send.at[part, d - 1, m],
            recv_sem=near_recv.at[part, d - 1, m],
            device_id={"tile": h * half + to},
        )

    def cross_copy(m):
        return pltpu.make_async_remote_copy(
            src_ref=crossing.at[pl.ds(m * step, step)],
            dst_ref=crossed.at[pl.ds(m * step, step)],
            send_sem=cross_send.at[m],
            recv_sem=cross_recv.at[m],
            device_id={"tile": (1 - h) * half + j},
        )

    def start_halo(k):
        pl.when(has_left)(lambda: tile_copy(k, True).start())
        pl.when(has_right)(lambda: tile_copy(k, False).start())
        pl.when(has_prev)(lambda: sec_copy(k, True).start())
        pl.when(has_next)(lambda: sec_copy(k, False).start())

    def wait_sec(k):
        @pl.when(has_prev)
        def _():
            sec_copy(k, False).wait_recv()

        @pl.when(has_next)
        def _():
            sec_copy(k, True).wait_recv()

    def wait_tile(k):
        @pl.when(has_left)
        def _():
            tile_copy(k, False).wait_recv()

        @pl.when(has_right)
        def _():
            tile_copy(k, True).wait_recv()

    def wait_sent(k):
        pl.when(has_left)(lambda: tile_copy(k, True).wait_send())
        pl.when(has_right)(lambda: tile_copy(k, False).wait_send())
        pl.when(has_prev)(lambda: sec_copy(k, True).wait_send())
        pl.when(has_next)(lambda: sec_copy(k, False).wait_send())

    load(3).wait()
    load(4).wait()
    for m in range(chunks):
        for s in range(m * step, (m + 1) * step):
            segment_sums(s)
        if m == 0:
            pl.semaphore_wait(barrier, partners)
        for d in range(1, half):
            near_copy(d, 0, m).start()
    load(0).wait()
    for s in range(secs):
        for c in range(comps):
            here = offsets[c, s]
            pos[0, s + 1, c] = here
            edge_out[0, 0, c * secs + s : c * secs + s + 1, :] = here[:1]
            edge_out[0, 1, c * secs + s : c * secs + s + 1, :] = here[rows - 1 :]
    start_halo(0)
    zero = jnp.zeros((rows, cols), jnp.float32)

    for k in range(ITERS):

        @pl.when(jnp.logical_not(has_prev))
        def _():
            for c in range(comps):
                pos[k, 0, c] = zero

        @pl.when(jnp.logical_not(has_next))
        def _():
            for c in range(comps):
                pos[k, secs + 1, c] = zero

        @pl.when(jnp.logical_not(has_left))
        def _():
            edge_in[k, 0] = jnp.zeros(edge_in.shape[2:], jnp.float32)

        @pl.when(jnp.logical_not(has_right))
        def _():
            edge_in[k, 1] = jnp.zeros(edge_in.shape[2:], jnp.float32)

    for i in (5, 6, 7, 8):
        load(i).wait()
    row_iota = lax.broadcasted_iota(jnp.int32, (rows, cols), 0)
    col_iota = lax.broadcasted_iota(jnp.int32, (rows, cols), 1)
    k_plane, k_cross = [], []
    for s in range(secs):
        kind = classes[s]
        plane, across = zero, zero
        for class_id in range(table.shape[1]):
            plane = jnp.where(kind == class_id, table[0:1, class_id : class_id + 1], plane)
            across = jnp.where(kind == class_id, table[1:2, class_id : class_id + 1], across)
        k_plane.append(plane)
        k_cross.append(across)

    def pulled(k, s, c, up):
        index = (match_up if up else match_down)[s]
        source = pos[k, s + 2 if up else s, c]
        return gather_nodes(source, index // cols, index % cols)

    def local_force(k, s, c):
        here = pos[k, s + 1, c]
        west = jnp.where(col_iota == 0, 0.0, pltpu.roll(here, 1, 1))
        east = jnp.where(col_iota == cols - 1, 0.0, pltpu.roll(here, cols - 1, 1))
        north = jnp.where(row_iota == 0, 0.0, pltpu.roll(here, 1, 0))
        south = jnp.where(row_iota == rows - 1, 0.0, pltpu.roll(here, rows - 1, 0))
        force = k_plane[s] * (west + east + north + south - 4.0 * here) - 2.0 * k_cross[s] * here
        if s < secs - 1:
            force = force + k_cross[s] * pulled(k, s, c, True)
        if s > 0:
            force = force + k_cross[s] * pulled(k, s, c, False)
        return force

    def sec_force(k, s, c):
        if s == secs - 1:
            force[s, c] = force[s, c] + k_cross[s] * pulled(k, s, c, True)
        if s == 0:
            force[s, c] = force[s, c] + k_cross[s] * pulled(k, s, c, False)

    def tile_force(k, s, c):
        line = c * secs + s
        north = jnp.where(row_iota == 0, edge_in[k, 0, line : line + 1, :], 0.0)
        south = jnp.where(row_iota == rows - 1, edge_in[k, 1, line : line + 1, :], 0.0)
        force[s, c] = force[s, c] + k_plane[s] * (north + south)

    nodes = [(s, c) for s in [0, secs - 1] + list(range(1, secs - 1)) for c in range(comps)]

    def halo_force(k):
        wait_sec(k)
        for s, c in nodes:
            sec_force(k, s, c)
        wait_tile(k)
        for s, c in nodes:
            tile_force(k, s, c)

    for k in range(ITERS):
        force = {(s, c): local_force(k, s, c) for s, c in nodes}
        if k == 0:
            for m in range(chunks):
                for d in range(1, half):
                    near_copy(d, 0, m).wait_recv()
                for s in range(m * step, (m + 1) * step):
                    for c in range(comps + 1):
                        total = dense[(1 - h) * half + j, s, c]
                        for d in range(1, half):
                            total = total + near_other[d - 1, s, c]
                        crossing[s, c] = total
                cross_copy(m).start()
            for m in range(chunks):
                for d in range(1, half):
                    near_copy(d, 1, m).start()
            halo_force(0)
            for m in range(chunks):
                for d in range(1, half):
                    near_copy(d, 1, m).wait_recv()
                cross_copy(m).wait_recv()
            flow_push, flow_hold = {}, {}
            for s in range(secs):
                sums = []
                for c in range(comps + 1):
                    total = dense[t, s, c] + crossed[s, c]
                    for d in range(1, half):
                        total = total + near_own[d - 1, s, c]
                    sums.append(total)
                scale = 1.0 / (1.0 + sums[comps])
                flow_hold[s] = sums[comps] * scale
                for c in range(comps):
                    flow_push[s, c] = sums[c] * scale
        else:
            force = {(s, c): force[s, c] + flow_push[s, c] - flow_hold[s] * pos[k, s + 1, c] for s, c in nodes}
            halo_force(k)
        for s, c in nodes:
            here = pos[k, s + 1, c]
            net = force[s, c]
            if k == 0:
                net = net + flow_push[s, c] - flow_hold[s] * here
            if k == ITERS - 1:
                net_out[c, s] = net
                vel_out[c, s] = vel[s, c]
                pos_out[c, s] = here
                continue
            speed = 0.5 * net if k == 0 else 0.9 * vel[s, c] + 0.5 * net
            moved = here + 0.5 * speed
            vel[s, c] = speed
            pos[k + 1, s + 1, c] = moved
            line = c * secs + s
            edge_out[k + 1, 0, line : line + 1, :] = moved[:1]
            edge_out[k + 1, 1, line : line + 1, :] = moved[rows - 1 :]
        if k < ITERS - 1:
            start_halo(k + 1)
        wait_sent(k)
        if k == 0:
            for m in range(chunks):
                for d in range(1, half):
                    near_copy(d, 0, m).wait_send()
                    near_copy(d, 1, m).wait_send()
                cross_copy(m).wait_send()


def shards(n_tile, n_sec, *args):
    offsets, flow_tiles, confidence, flow_owner, flow_row = args[:5]
    match_up, match_down, classes, spring_table = args[5:]
    comps, secs, rows, cols = offsets.shape
    flows = confidence.shape[1]
    half = n_tile // 2
    block = (secs, comps + 1, rows, cols)
    vmem = pl.BlockSpec(memory_space=pltpu.VMEM)
    f32 = jnp.float32
    dma = pltpu.SemaphoreType.DMA
    chunks = min(CHUNKS, secs)
    operands = (
        offsets,
        flow_tiles.reshape(secs, flows * comps, cols),
        confidence,
        flow_owner.reshape(secs, flows),
        flow_row,
        match_up.reshape(secs, rows, cols),
        match_down.reshape(secs, rows, cols),
        classes,
        spring_table,
    )
    net, velocity, position = pl.pallas_call(
        functools.partial(kernel, n_tile, n_sec),
        out_shape=(pltpu.VMEM(offsets.shape, f32),) * 3,
        in_specs=[pl.BlockSpec(memory_space=pltpu.HBM)] * 9,
        out_specs=(vmem, vmem, vmem),
        scratch_shapes=[pltpu.VMEM(x.shape, x.dtype) for x in operands]
        + [
            pltpu.VMEM((n_tile,) + block, f32),
            pltpu.VMEM((half - 1,) + block, f32),
            pltpu.VMEM((half - 1,) + block, f32),
            pltpu.VMEM(block, f32),
            pltpu.VMEM(block, f32),
            pltpu.VMEM((ITERS, secs + 2, comps, rows, cols), f32),
            pltpu.VMEM((secs, comps, rows, cols), f32),
            pltpu.VMEM((ITERS, 2, comps * secs, cols), f32),
            pltpu.VMEM((ITERS, 2, comps * secs, cols), f32),
            dma((2, half - 1, chunks)),
            dma((2, half - 1, chunks)),
            dma((chunks,)),
            dma((chunks,)),
            dma((ITERS, 2)),
            dma((ITERS, 2)),
            dma((ITERS, 2)),
            dma((ITERS, 2)),
            dma((9,)),
            dma((2, secs)),
        ],
        compiler_params=pltpu.CompilerParams(
            collective_id=0, has_side_effects=True, vmem_limit_bytes=63 * 1024 * 1024
        ),
    )(*operands)
    velocity = 0.9 * velocity + 0.5 * net
    return position + 0.5 * velocity, velocity


def solution(mesh):
    placed = (
        P(None, "sec", "tile", None),
        P("sec", "tile", None, None),
        P("sec", "tile", None),
        P("sec", "tile", None),
        P("sec", "tile"),
        P("sec", "tile", None),
        P("sec", "tile", None),
        P("sec", "tile", None),
        P(),
    )
    return jax.shard_map(
        functools.partial(shards, mesh.shape["tile"], mesh.shape["sec"]),
        mesh=mesh,
        in_specs=placed,
        out_specs=(P(None, "sec", "tile", None), P(None, "sec", "tile", None)),
        check_vma=False,
    )
```

```python
import functools

import jax
import jax.numpy as jnp
from jax import lax
from jax.experimental import pallas as pl
from jax.experimental.pallas import tpu as pltpu
from jax.sharding import PartitionSpec as P

ITERS = 3
CHUNKS = 1


def gather_nodes(source, row, col):
    rows = source.shape[0]
    picked = None
    for r in range(rows):
        line = jnp.broadcast_to(source[r : r + 1, :], source.shape)
        taken = jnp.take_along_axis(line, col, axis=1)
        picked = taken if r == 0 else jnp.where(row == r, taken, picked)
    return picked


def kernel(
    n_tile,
    n_sec,
    *refs,
):
    in_hbm, outs, staged = refs[:9], refs[9:12], refs[12:21]
    offsets, flow, conf, owner, flow_row, match_up, match_down, classes, table = staged
    net_out, vel_out, pos_out = outs
    dense, near_other, near_own, crossing, crossed, pos, vel, edge_out, edge_in = refs[21:30]
    near_send, near_recv, cross_send, cross_recv = refs[30:34]
    tile_send, tile_recv, sec_send, sec_recv, load_sem = refs[34:]
    comps, secs, rows, cols = offsets.shape
    flows = conf.shape[1]
    half = n_tile // 2
    t = lax.axis_index("tile")
    s_me = lax.axis_index("sec")
    h, j = t // half, t % half

    chunks = min(CHUNKS, secs)
    step = secs // chunks

    def load(i):
        return pltpu.make_async_copy(in_hbm[i], staged[i], load_sem.at[i])

    load(3).start()
    load(4).start()
    load(1).start()
    load(2).start()

    barrier = pltpu.get_barrier_semaphore()
    has_prev, has_next = s_me > 0, s_me < n_sec - 1
    has_left, has_right = t > 0, t < n_tile - 1

    for d in range(1, half):
        pl.semaphore_signal(barrier, inc=1, device_id={"tile": h * half + (j + d) % half})
    pl.semaphore_signal(barrier, inc=1, device_id={"tile": (1 - h) * half + j})
    over_right = jnp.logical_and(t == half - 1, half > 1)
    over_left = jnp.logical_and(t == half, half > 1)

    def greet(there, partner):
        @pl.when(there)
        def _():
            pl.semaphore_signal(barrier, inc=1, device_id=partner)

    greet(has_prev, {"sec": s_me - 1})
    greet(has_next, {"sec": s_me + 1})
    greet(over_right, {"tile": t + 1})
    greet(over_left, {"tile": t - 1})
    partners = half
    for there in (has_prev, has_next, over_right, over_left):
        partners = partners + there.astype(jnp.int32)

    key_iota = lax.broadcasted_iota(jnp.int32, (n_tile * rows, flows), 0)

    def segment_sums(s):
        key = owner[s : s + 1, :] * rows + flow_row[s : s + 1, :]
        hit = (jnp.broadcast_to(key, key_iota.shape) == key_iota).astype(jnp.float32)
        hit = hit.astype(jnp.bfloat16)
        w = conf[s]
        parts = [w * flow[s, pl.ds(c, flows, stride=comps), :] for c in range(comps)] + [w]
        payload = jnp.concatenate(parts, axis=1)
        high = payload.astype(jnp.bfloat16)
        low = (payload - high.astype(jnp.float32)).astype(jnp.bfloat16)
        both = jnp.concatenate([high, low], axis=0)
        hit2 = jnp.concatenate([hit, hit], axis=1)
        sums = jnp.dot(hit2, both, preferred_element_type=jnp.float32)
        for o in range(n_tile):
            for c in range(comps + 1):
                dense[o, s, c] = sums[o * rows : (o + 1) * rows, c * cols : (c + 1) * cols]

    def sec_copy(k, up):
        return pltpu.make_async_remote_copy(
            src_ref=pos.at[k, 1 if up else secs],
            dst_ref=pos.at[k, secs + 1 if up else 0],
            send_sem=sec_send.at[k, 0 if up else 1],
            recv_sem=sec_recv.at[k, 0 if up else 1],
            device_id={"sec": s_me - 1 if up else s_me + 1},
        )

    def tile_copy(k, up):
        return pltpu.make_async_remote_copy(
            src_ref=edge_out.at[k, 0 if up else 1],
            dst_ref=edge_in.at[k, 1 if up else 0],
            send_sem=tile_send.at[k, 0 if up else 1],
            recv_sem=tile_recv.at[k, 0 if up else 1],
            device_id={"tile": t - 1 if up else t + 1},
        )

    def near_copy(d, part, m):
        to = (j + d) % half
        source = dense.at[(1 - h if part == 0 else h) * half + to]
        landing = near_other if part == 0 else near_own
        return pltpu.make_async_remote_copy(
            src_ref=source.at[pl.ds(m * step, step)],
            dst_ref=landing.at[d - 1, pl.ds(m * step, step)],
            send_sem=near_send.at[part, d - 1, m],
            recv_sem=near_recv.at[part, d - 1, m],
            device_id={"tile": h * half + to},
        )

    def cross_copy(m):
        return pltpu.make_async_remote_copy(
            src_ref=crossing.at[pl.ds(m * step, step)],
            dst_ref=crossed.at[pl.ds(m * step, step)],
            send_sem=cross_send.at[m],
            recv_sem=cross_recv.at[m],
            device_id={"tile": (1 - h) * half + j},
        )

    def start_halo(k):
        pl.when(has_left)(lambda: tile_copy(k, True).start())
        pl.when(has_right)(lambda: tile_copy(k, False).start())
        pl.when(has_prev)(lambda: sec_copy(k, True).start())
        pl.when(has_next)(lambda: sec_copy(k, False).start())

    def wait_sec(k):
        @pl.when(has_prev)
        def _():
            sec_copy(k, False).wait_recv()

        @pl.when(has_next)
        def _():
            sec_copy(k, True).wait_recv()

    def wait_tile(k):
        @pl.when(has_left)
        def _():
            tile_copy(k, False).wait_recv()

        @pl.when(has_right)
        def _():
            tile_copy(k, True).wait_recv()

    def wait_sent(k):
        pl.when(has_left)(lambda: tile_copy(k, True).wait_send())
        pl.when(has_right)(lambda: tile_copy(k, False).wait_send())
        pl.when(has_prev)(lambda: sec_copy(k, True).wait_send())
        pl.when(has_next)(lambda: sec_copy(k, False).wait_send())

    for i in (0, 5, 6, 7, 8):
        load(i).start()
    for i in (3, 4, 1, 2):
        load(i).wait()
    for m in range(chunks):
        for s in range(m * step, (m + 1) * step):
            segment_sums(s)
        if m == 0:
            pl.semaphore_wait(barrier, partners)
        for d in list(range(1, half, 2)) + list(range(2, half, 2)):
            near_copy(d, 0, m).start()
    load(0).wait()
    for s in range(secs):
        for c in range(comps):
            here = offsets[c, s]
            pos[0, s + 1, c] = here
            edge_out[0, 0, c * secs + s : c * secs + s + 1, :] = here[:1]
            edge_out[0, 1, c * secs + s : c * secs + s + 1, :] = here[rows - 1 :]
    start_halo(0)
    zero = jnp.zeros((rows, cols), jnp.float32)

    for k in range(ITERS):

        @pl.when(jnp.logical_not(has_prev))
        def _():
            for c in range(comps):
                pos[k, 0, c] = zero

        @pl.when(jnp.logical_not(has_next))
        def _():
            for c in range(comps):
                pos[k, secs + 1, c] = zero

        @pl.when(jnp.logical_not(has_left))
        def _():
            edge_in[k, 0] = jnp.zeros(edge_in.shape[2:], jnp.float32)

        @pl.when(jnp.logical_not(has_right))
        def _():
            edge_in[k, 1] = jnp.zeros(edge_in.shape[2:], jnp.float32)

    for i in (5, 6, 7, 8):
        load(i).wait()
    row_iota = lax.broadcasted_iota(jnp.int32, (rows, cols), 0)
    col_iota = lax.broadcasted_iota(jnp.int32, (rows, cols), 1)
    k_plane, k_cross = [], []
    for s in range(secs):
        kind = classes[s]
        plane, across = zero, zero
        for class_id in range(table.shape[1]):
            plane = jnp.where(kind == class_id, table[0:1, class_id : class_id + 1], plane)
            across = jnp.where(kind == class_id, table[1:2, class_id : class_id + 1], across)
        k_plane.append(plane)
        k_cross.append(across)

    def pulled(k, s, c, up):
        index = (match_up if up else match_down)[s]
        source = pos[k, s + 2 if up else s, c]
        return gather_nodes(source, index // cols, index % cols)

    def local_force(k, s, c):
        here = pos[k, s + 1, c]
        west = jnp.where(col_iota == 0, 0.0, pltpu.roll(here, 1, 1))
        east = jnp.where(col_iota == cols - 1, 0.0, pltpu.roll(here, cols - 1, 1))
        north = jnp.where(row_iota == 0, 0.0, pltpu.roll(here, 1, 0))
        south = jnp.where(row_iota == rows - 1, 0.0, pltpu.roll(here, rows - 1, 0))
        force = k_plane[s] * (west + east + north + south - 4.0 * here) - 2.0 * k_cross[s] * here
        if s < secs - 1:
            force = force + k_cross[s] * pulled(k, s, c, True)
        if s > 0:
            force = force + k_cross[s] * pulled(k, s, c, False)
        return force

    def sec_force(k, s, c):
        if s == secs - 1:
            force[s, c] = force[s, c] + k_cross[s] * pulled(k, s, c, True)
        if s == 0:
            force[s, c] = force[s, c] + k_cross[s] * pulled(k, s, c, False)

    def tile_force(k, s, c):
        line = c * secs + s
        north = jnp.where(row_iota == 0, edge_in[k, 0, line : line + 1, :], 0.0)
        south = jnp.where(row_iota == rows - 1, edge_in[k, 1, line : line + 1, :], 0.0)
        force[s, c] = force[s, c] + k_plane[s] * (north + south)

    nodes = [(s, c) for s in [0, secs - 1] + list(range(1, secs - 1)) for c in range(comps)]

    def halo_force(k):
        wait_sec(k)
        for s, c in nodes:
            sec_force(k, s, c)
        wait_tile(k)
        for s, c in nodes:
            tile_force(k, s, c)

    for k in range(ITERS):
        force = {(s, c): local_force(k, s, c) for s, c in nodes}
        if k == 0:
            for m in range(chunks):
                for d in range(1, half):
                    near_copy(d, 0, m).wait_recv()
                for s in range(m * step, (m + 1) * step):
                    for c in range(comps + 1):
                        total = dense[(1 - h) * half + j, s, c]
                        for d in range(1, half):
                            total = total + near_other[d - 1, s, c]
                        crossing[s, c] = total
                cross_copy(m).start()
            for m in range(chunks):
                for d in range(1, half):
                    near_copy(d, 1, m).start()
            halo_force(0)
            for m in range(chunks):
                for d in range(1, half):
                    near_copy(d, 1, m).wait_recv()
                cross_copy(m).wait_recv()
            flow_push, flow_hold = {}, {}
            for s in range(secs):
                sums = []
                for c in range(comps + 1):
                    total = dense[t, s, c] + crossed[s, c]
                    for d in range(1, half):
                        total = total + near_own[d - 1, s, c]
                    sums.append(total)
                scale = 1.0 / (1.0 + sums[comps])
                flow_hold[s] = sums[comps] * scale
                for c in range(comps):
                    flow_push[s, c] = sums[c] * scale
        else:
            force = {(s, c): force[s, c] + flow_push[s, c] - flow_hold[s] * pos[k, s + 1, c] for s, c in nodes}
            halo_force(k)
        for s, c in nodes:
            here = pos[k, s + 1, c]
            net = force[s, c]
            if k == 0:
                net = net + flow_push[s, c] - flow_hold[s] * here
            if k == ITERS - 1:
                net_out[c, s] = net
                vel_out[c, s] = vel[s, c]
                pos_out[c, s] = here
                continue
            speed = 0.5 * net if k == 0 else 0.9 * vel[s, c] + 0.5 * net
            moved = here + 0.5 * speed
            vel[s, c] = speed
            pos[k + 1, s + 1, c] = moved
            line = c * secs + s
            edge_out[k + 1, 0, line : line + 1, :] = moved[:1]
            edge_out[k + 1, 1, line : line + 1, :] = moved[rows - 1 :]
        if k < ITERS - 1:
            start_halo(k + 1)
        wait_sent(k)
        if k == 0:
            for m in range(chunks):
                for d in range(1, half):
                    near_copy(d, 0, m).wait_send()
                    near_copy(d, 1, m).wait_send()
                cross_copy(m).wait_send()


def shards(n_tile, n_sec, *args):
    offsets, flow_tiles, confidence, flow_owner, flow_row = args[:5]
    match_up, match_down, classes, spring_table = args[5:]
    comps, secs, rows, cols = offsets.shape
    flows = confidence.shape[1]
    half = n_tile // 2
    block = (secs, comps + 1, rows, cols)
    vmem = pl.BlockSpec(memory_space=pltpu.VMEM)
    f32 = jnp.float32
    dma = pltpu.SemaphoreType.DMA
    chunks = min(CHUNKS, secs)
    operands = (
        offsets,
        flow_tiles.reshape(secs, flows * comps, cols),
        confidence,
        flow_owner.reshape(secs, flows),
        flow_row,
        match_up.reshape(secs, rows, cols),
        match_down.reshape(secs, rows, cols),
        classes,
        spring_table,
    )
    net, velocity, position = pl.pallas_call(
        functools.partial(kernel, n_tile, n_sec),
        out_shape=(pltpu.VMEM(offsets.shape, f32),) * 3,
        in_specs=[pl.BlockSpec(memory_space=pltpu.HBM)] * 9,
        out_specs=(vmem, vmem, vmem),
        scratch_shapes=[pltpu.VMEM(x.shape, x.dtype) for x in operands]
        + [
            pltpu.VMEM((n_tile,) + block, f32),
            pltpu.VMEM((half - 1,) + block, f32),
            pltpu.VMEM((half - 1,) + block, f32),
            pltpu.VMEM(block, f32),
            pltpu.VMEM(block, f32),
            pltpu.VMEM((ITERS, secs + 2, comps, rows, cols), f32),
            pltpu.VMEM((secs, comps, rows, cols), f32),
            pltpu.VMEM((ITERS, 2, comps * secs, cols), f32),
            pltpu.VMEM((ITERS, 2, comps * secs, cols), f32),
            dma((2, half - 1, chunks)),
            dma((2, half - 1, chunks)),
            dma((chunks,)),
            dma((chunks,)),
            dma((ITERS, 2)),
            dma((ITERS, 2)),
            dma((ITERS, 2)),
            dma((ITERS, 2)),
            dma((9,)),
        ],
        compiler_params=pltpu.CompilerParams(
            collective_id=0, has_side_effects=True, vmem_limit_bytes=63 * 1024 * 1024
        ),
    )(*operands)
    velocity = 0.9 * velocity + 0.5 * net
    return position + 0.5 * velocity, velocity


def solution(mesh):
    placed = (
        P(None, "sec", "tile", None),
        P("sec", "tile", None, None),
        P("sec", "tile", None),
        P("sec", "tile", None),
        P("sec", "tile"),
        P("sec", "tile", None),
        P("sec", "tile", None),
        P("sec", "tile", None),
        P(),
    )
    return jax.shard_map(
        functools.partial(shards, mesh.shape["tile"], mesh.shape["sec"]),
        mesh=mesh,
        in_specs=placed,
        out_specs=(P(None, "sec", "tile", None), P(None, "sec", "tile", None)),
        check_vma=False,
    )
```

```python
import functools

import jax
import jax.numpy as jnp
from jax import lax
from jax.experimental import pallas as pl
from jax.experimental.pallas import tpu as pltpu
from jax.sharding import PartitionSpec as P

ITERS = 3
CHUNKS = 1


def gather_nodes(source, row, col):
    rows = source.shape[0]
    picked = None
    for r in range(rows):
        line = jnp.broadcast_to(source[r : r + 1, :], source.shape)
        taken = jnp.take_along_axis(line, col, axis=1)
        picked = taken if r == 0 else jnp.where(row == r, taken, picked)
    return picked


def kernel(
    n_tile,
    n_sec,
    *refs,
):
    in_hbm, outs, staged = refs[:9], refs[9:12], refs[12:21]
    offsets, flow, conf, owner, flow_row, match_up, match_down, classes, table = staged
    net_out, vel_out, pos_out = outs
    dense, near_other, near_own, crossing, crossed, pos, vel, edge_out, edge_in = refs[21:30]
    near_send, near_recv, cross_send, cross_recv = refs[30:34]
    tile_send, tile_recv, sec_send, sec_recv, load_sem = refs[34:]
    comps, secs, rows, cols = offsets.shape
    flows = conf.shape[1]
    half = n_tile // 2
    t = lax.axis_index("tile")
    s_me = lax.axis_index("sec")
    h, j = t // half, t % half

    chunks = min(CHUNKS, secs)
    step = secs // chunks

    def load(i):
        return pltpu.make_async_copy(in_hbm[i], staged[i], load_sem.at[i])

    load(3).start()
    load(4).start()
    load(1).start()
    load(2).start()

    barrier = pltpu.get_barrier_semaphore()
    has_prev, has_next = s_me > 0, s_me < n_sec - 1
    has_left, has_right = t > 0, t < n_tile - 1

    for d in range(1, half):
        pl.semaphore_signal(barrier, inc=1, device_id={"tile": h * half + (j + d) % half})
    pl.semaphore_signal(barrier, inc=1, device_id={"tile": (1 - h) * half + j})
    over_right = jnp.logical_and(t == half - 1, half > 1)
    over_left = jnp.logical_and(t == half, half > 1)

    def greet(there, partner):
        @pl.when(there)
        def _():
            pl.semaphore_signal(barrier, inc=1, device_id=partner)

    greet(has_prev, {"sec": s_me - 1})
    greet(has_next, {"sec": s_me + 1})
    greet(over_right, {"tile": t + 1})
    greet(over_left, {"tile": t - 1})
    partners = half
    for there in (has_prev, has_next, over_right, over_left):
        partners = partners + there.astype(jnp.int32)

    key_iota = lax.broadcasted_iota(jnp.int32, (n_tile * rows, flows), 0)

    def segment_sums(s):
        key = owner[s : s + 1, :] * rows + flow_row[s : s + 1, :]
        hit = (jnp.broadcast_to(key, key_iota.shape) == key_iota).astype(jnp.float32)
        hit = hit.astype(jnp.bfloat16)
        w = conf[s]
        parts = [w * flow[s, pl.ds(c, flows, stride=comps), :] for c in range(comps)] + [w]
        payload = jnp.concatenate(parts, axis=1)
        high = payload.astype(jnp.bfloat16)
        low = (payload - high.astype(jnp.float32)).astype(jnp.bfloat16)
        both = jnp.concatenate([high, low], axis=0)
        hit2 = jnp.concatenate([hit, hit], axis=1)
        sums = jnp.dot(hit2, both, preferred_element_type=jnp.float32)
        for o in range(n_tile):
            for c in range(comps + 1):
                dense[o, s, c] = sums[o * rows : (o + 1) * rows, c * cols : (c + 1) * cols]

    def sec_copy(k, up):
        return pltpu.make_async_remote_copy(
            src_ref=pos.at[k, 1 if up else secs],
            dst_ref=pos.at[k, secs + 1 if up else 0],
            send_sem=sec_send.at[k, 0 if up else 1],
            recv_sem=sec_recv.at[k, 0 if up else 1],
            device_id={"sec": s_me - 1 if up else s_me + 1},
        )

    def tile_copy(k, up):
        return pltpu.make_async_remote_copy(
            src_ref=edge_out.at[k, 0 if up else 1],
            dst_ref=edge_in.at[k, 1 if up else 0],
            send_sem=tile_send.at[k, 0 if up else 1],
            recv_sem=tile_recv.at[k, 0 if up else 1],
            device_id={"tile": t - 1 if up else t + 1},
        )

    def near_copy(d, part, m):
        to = (j + d) % half
        source = dense.at[(1 - h if part == 0 else h) * half + to]
        landing = near_other if part == 0 else near_own
        return pltpu.make_async_remote_copy(
            src_ref=source.at[pl.ds(m * step, step)],
            dst_ref=landing.at[d - 1, pl.ds(m * step, step)],
            send_sem=near_send.at[part, d - 1, m],
            recv_sem=near_recv.at[part, d - 1, m],
            device_id={"tile": h * half + to},
        )

    def cross_copy(m):
        return pltpu.make_async_remote_copy(
            src_ref=crossing.at[pl.ds(m * step, step)],
            dst_ref=crossed.at[pl.ds(m * step, step)],
            send_sem=cross_send.at[m],
            recv_sem=cross_recv.at[m],
            device_id={"tile": (1 - h) * half + j},
        )

    def start_tile(k):
        pl.when(has_left)(lambda: tile_copy(k, True).start())
        pl.when(has_right)(lambda: tile_copy(k, False).start())

    def start_sec(k):
        pl.when(has_prev)(lambda: sec_copy(k, True).start())
        pl.when(has_next)(lambda: sec_copy(k, False).start())

    def wait_sec(k):
        @pl.when(has_prev)
        def _():
            sec_copy(k, False).wait_recv()

        @pl.when(has_next)
        def _():
            sec_copy(k, True).wait_recv()

    def wait_tile(k):
        @pl.when(has_left)
        def _():
            tile_copy(k, False).wait_recv()

        @pl.when(has_right)
        def _():
            tile_copy(k, True).wait_recv()

    def wait_sent(k):
        pl.when(has_left)(lambda: tile_copy(k, True).wait_send())
        pl.when(has_right)(lambda: tile_copy(k, False).wait_send())
        pl.when(has_prev)(lambda: sec_copy(k, True).wait_send())
        pl.when(has_next)(lambda: sec_copy(k, False).wait_send())

    for i in (0, 5, 6, 7, 8):
        load(i).start()
    for i in (3, 4, 1, 2):
        load(i).wait()
    for m in range(chunks):
        for s in range(m * step, (m + 1) * step):
            segment_sums(s)
        if m == 0:
            pl.semaphore_wait(barrier, partners)
        for d in list(range(1, half, 2)) + list(range(2, half, 2)):
            near_copy(d, 0, m).start()
    load(0).wait()
    for s in range(secs):
        for c in range(comps):
            here = offsets[c, s]
            pos[0, s + 1, c] = here
            edge_out[0, 0, c * secs + s : c * secs + s + 1, :] = here[:1]
            edge_out[0, 1, c * secs + s : c * secs + s + 1, :] = here[rows - 1 :]
    start_tile(0)
    start_sec(0)
    zero = jnp.zeros((rows, cols), jnp.float32)

    for k in range(ITERS):

        @pl.when(jnp.logical_not(has_prev))
        def _():
            for c in range(comps):
                pos[k, 0, c] = zero

        @pl.when(jnp.logical_not(has_next))
        def _():
            for c in range(comps):
                pos[k, secs + 1, c] = zero

        @pl.when(jnp.logical_not(has_left))
        def _():
            edge_in[k, 0] = jnp.zeros(edge_in.shape[2:], jnp.float32)

        @pl.when(jnp.logical_not(has_right))
        def _():
            edge_in[k, 1] = jnp.zeros(edge_in.shape[2:], jnp.float32)

    for i in (5, 6, 7, 8):
        load(i).wait()
    row_iota = lax.broadcasted_iota(jnp.int32, (rows, cols), 0)
    col_iota = lax.broadcasted_iota(jnp.int32, (rows, cols), 1)
    k_plane, k_cross = [], []
    for s in range(secs):
        kind = classes[s]
        plane, across = zero, zero
        for class_id in range(table.shape[1]):
            plane = jnp.where(kind == class_id, table[0:1, class_id : class_id + 1], plane)
            across = jnp.where(kind == class_id, table[1:2, class_id : class_id + 1], across)
        k_plane.append(plane)
        k_cross.append(across)

    def pulled(k, s, c, up):
        index = (match_up if up else match_down)[s]
        source = pos[k, s + 2 if up else s, c]
        return gather_nodes(source, index // cols, index % cols)

    def local_force(k, s, c):
        here = pos[k, s + 1, c]
        west = jnp.where(col_iota == 0, 0.0, pltpu.roll(here, 1, 1))
        east = jnp.where(col_iota == cols - 1, 0.0, pltpu.roll(here, cols - 1, 1))
        north = jnp.where(row_iota == 0, 0.0, pltpu.roll(here, 1, 0))
        south = jnp.where(row_iota == rows - 1, 0.0, pltpu.roll(here, rows - 1, 0))
        force = k_plane[s] * (west + east + north + south - 4.0 * here) - 2.0 * k_cross[s] * here
        if s < secs - 1:
            force = force + k_cross[s] * pulled(k, s, c, True)
        if s > 0:
            force = force + k_cross[s] * pulled(k, s, c, False)
        return force

    def sec_force(k, s, c):
        if s == secs - 1:
            force[s, c] = force[s, c] + k_cross[s] * pulled(k, s, c, True)
        if s == 0:
            force[s, c] = force[s, c] + k_cross[s] * pulled(k, s, c, False)

    def tile_force(k, s, c):
        line = c * secs + s
        north = jnp.where(row_iota == 0, edge_in[k, 0, line : line + 1, :], 0.0)
        south = jnp.where(row_iota == rows - 1, edge_in[k, 1, line : line + 1, :], 0.0)
        force[s, c] = force[s, c] + k_plane[s] * (north + south)

    nodes = [(s, c) for s in [0, secs - 1] + list(range(1, secs - 1)) for c in range(comps)]

    def halo_force(k):
        wait_sec(k)
        for s, c in nodes:
            sec_force(k, s, c)
        wait_tile(k)
        for s, c in nodes:
            tile_force(k, s, c)

    for k in range(ITERS):
        force = {(s, c): local_force(k, s, c) for s, c in nodes}
        if k == 0:
            for m in range(chunks):
                for d in range(1, half):
                    near_copy(d, 0, m).wait_recv()
                for s in range(m * step, (m + 1) * step):
                    for c in range(comps + 1):
                        total = dense[(1 - h) * half + j, s, c]
                        for d in range(1, half):
                            total = total + near_other[d - 1, s, c]
                        crossing[s, c] = total
                cross_copy(m).start()
            for m in range(chunks):
                for d in range(1, half):
                    near_copy(d, 1, m).start()
            halo_force(0)
            for m in range(chunks):
                for d in range(1, half):
                    near_copy(d, 1, m).wait_recv()
                cross_copy(m).wait_recv()
            flow_push, flow_hold = {}, {}
            for s in range(secs):
                sums = []
                for c in range(comps + 1):
                    total = dense[t, s, c] + crossed[s, c]
                    for d in range(1, half):
                        total = total + near_own[d - 1, s, c]
                    sums.append(total)
                scale = 1.0 / (1.0 + sums[comps])
                flow_hold[s] = sums[comps] * scale
                for c in range(comps):
                    flow_push[s, c] = sums[c] * scale
        else:
            force = {(s, c): force[s, c] + flow_push[s, c] - flow_hold[s] * pos[k, s + 1, c] for s, c in nodes}
            halo_force(k)
        later = {}
        for s, c in nodes:
            here = pos[k, s + 1, c]
            net = force[s, c]
            if k == 0:
                net = net + flow_push[s, c] - flow_hold[s] * here
            if k == ITERS - 1:
                net_out[c, s] = net
                vel_out[c, s] = vel[s, c]
                pos_out[c, s] = here
                continue
            speed = 0.5 * net if k == 0 else 0.9 * vel[s, c] + 0.5 * net
            moved = here + 0.5 * speed
            later[s, c] = (speed, moved)
            line = c * secs + s
            edge_out[k + 1, 0, line : line + 1, :] = moved[:1]
            edge_out[k + 1, 1, line : line + 1, :] = moved[rows - 1 :]
        if k < ITERS - 1:
            start_tile(k + 1)
            for s, c in nodes:
                vel[s, c], pos[k + 1, s + 1, c] = later[s, c]
            start_sec(k + 1)
        wait_sent(k)
        if k == 0:
            for m in range(chunks):
                for d in range(1, half):
                    near_copy(d, 0, m).wait_send()
                    near_copy(d, 1, m).wait_send()
                cross_copy(m).wait_send()


def shards(n_tile, n_sec, *args):
    offsets, flow_tiles, confidence, flow_owner, flow_row = args[:5]
    match_up, match_down, classes, spring_table = args[5:]
    comps, secs, rows, cols = offsets.shape
    flows = confidence.shape[1]
    half = n_tile // 2
    block = (secs, comps + 1, rows, cols)
    vmem = pl.BlockSpec(memory_space=pltpu.VMEM)
    f32 = jnp.float32
    dma = pltpu.SemaphoreType.DMA
    chunks = min(CHUNKS, secs)
    operands = (
        offsets,
        flow_tiles.reshape(secs, flows * comps, cols),
        confidence,
        flow_owner.reshape(secs, flows),
        flow_row,
        match_up.reshape(secs, rows, cols),
        match_down.reshape(secs, rows, cols),
        classes,
        spring_table,
    )
    net, velocity, position = pl.pallas_call(
        functools.partial(kernel, n_tile, n_sec),
        out_shape=(pltpu.VMEM(offsets.shape, f32),) * 3,
        in_specs=[pl.BlockSpec(memory_space=pltpu.HBM)] * 9,
        out_specs=(vmem, vmem, vmem),
        scratch_shapes=[pltpu.VMEM(x.shape, x.dtype) for x in operands]
        + [
            pltpu.VMEM((n_tile,) + block, f32),
            pltpu.VMEM((half - 1,) + block, f32),
            pltpu.VMEM((half - 1,) + block, f32),
            pltpu.VMEM(block, f32),
            pltpu.VMEM(block, f32),
            pltpu.VMEM((ITERS, secs + 2, comps, rows, cols), f32),
            pltpu.VMEM((secs, comps, rows, cols), f32),
            pltpu.VMEM((ITERS, 2, comps * secs, cols), f32),
            pltpu.VMEM((ITERS, 2, comps * secs, cols), f32),
            dma((2, half - 1, chunks)),
            dma((2, half - 1, chunks)),
            dma((chunks,)),
            dma((chunks,)),
            dma((ITERS, 2)),
            dma((ITERS, 2)),
            dma((ITERS, 2)),
            dma((ITERS, 2)),
            dma((9,)),
        ],
        compiler_params=pltpu.CompilerParams(
            collective_id=0, has_side_effects=True, vmem_limit_bytes=63 * 1024 * 1024
        ),
    )(*operands)
    velocity = 0.9 * velocity + 0.5 * net
    return position + 0.5 * velocity, velocity


def solution(mesh):
    placed = (
        P(None, "sec", "tile", None),
        P("sec", "tile", None, None),
        P("sec", "tile", None),
        P("sec", "tile", None),
        P("sec", "tile"),
        P("sec", "tile", None),
        P("sec", "tile", None),
        P("sec", "tile", None),
        P(),
    )
    return jax.shard_map(
        functools.partial(shards, mesh.shape["tile"], mesh.shape["sec"]),
        mesh=mesh,
        in_specs=placed,
        out_specs=(P(None, "sec", "tile", None), P(None, "sec", "tile", None)),
        check_vma=False,
    )
```
